32 devices in a mesh: node: 8 (over z, x), freq: 4 (over y, core).
Axes of the slice: x: 2, y: 2, z: 4, core: 2. Of those that a mesh axis runs over, the one named last changes fastest.
Arguments:
- receiver_gathers: float32 [256, 393216], P('node', 'freq'), may hold values from -6 to 6
- fourier_estimate: float32 [64, 2, 256, 384], P(('node', 'freq')), may hold values from -6 to 6
- random_projector: float32 [384, 48], replicated, may hold values from -0.3125 to 0.3125
- release_sample: int32 [384], P('freq'), may hold values from 0 to 393215, as said below
Outputs:
- deblended: float32 [64, 2, 256, 384], P(('node', 'freq'))
- misfit_signal: float32 [256, 393216], P('node', 'freq')
The draws below stay inside these ranges and needn't reach their ends.
Inputs may be any that keep to these rules, and one draw needn't show every extreme that they name: `release_sample`: shot s fires at a sample of [s * 1024, (s + 1) * 1024).
All inputs are finite; a program needn't handle non-finite values.
Results may differ from the reference program's by a relative error of at most 0.0003.
Values sent between devices are 32-bit elements; how exact they have to be, the bound alone decides.
A program may use at most 192 MiB of HBM per device.

```python
import math
from functools import partial
import jax
import jax.numpy as jnp
from jax import lax

SOURCE_COUNT = 384
RECEIVER_COUNT = 256
LISTEN_SPAN = 4096
SOURCE_SPACING = 1024
RANK = 48
FREQS = 64
LENGTH = 393216


def draw_release_sample(key, part):
    random_dither = jax.random.randint(jax.random.fold_in(key, 17), (SOURCE_COUNT,), 0, SOURCE_SPACING, dtype=jnp.int32)
    return jnp.arange(SOURCE_COUNT, dtype=jnp.int32) * SOURCE_SPACING + random_dither


def level_of(key, dims, pieces, low, top_value):
    factor_of = 1.0
    for dim, blocks in pieces:
        steps = jax.random.uniform(jax.random.fold_in(jax.random.fold_in(key, 6), dim), (blocks,), jnp.float32, low / len(pieces), top_value / len(pieces))
        factor_of = factor_of * jnp.repeat(jnp.exp(steps), dims[dim] // blocks).reshape((-1,) + (1,) * (len(dims) - 1 - dim))
    return factor_of


def centred(own_key, dims, width, most, shards=(), held_as=jnp.bfloat16):
    entries = jax.random.normal(own_key, dims, jnp.float32) * width
    if len(shards) > 0:
        entries = level_of(own_key, dims, shards, -0.22, 0.18) * entries
    return jnp.clip(entries, min=-most, max=most).astype(held_as)


def setup_inputs(seed: int = 0) -> dict:
    splits = jax.random.split(jax.random.key(seed), 5)
    receiver_gathers = centred(splits[0], (RECEIVER_COUNT, LENGTH), 1.0, 6.0, ((0, 8), (1, 4)), jnp.float32)
    fourier_estimate = centred(splits[1], (FREQS, 2, RECEIVER_COUNT, SOURCE_COUNT), 1.0, 6.0, ((0, 32),), jnp.float32)
    random_projector = centred(splits[2], (SOURCE_COUNT, RANK), SOURCE_COUNT ** -0.5, 0.3125, (), jnp.float32)
    release_sample = draw_release_sample(jax.random.fold_in(splits[4], 71), 0)
    return {"receiver_gathers": receiver_gathers, "fourier_estimate": fourier_estimate, "random_projector": random_projector, "release_sample": release_sample}


relaxation = 0.25
ridge_scale = 0.001
highest = lax.Precision.HIGHEST

def dft_table(bin_count, length):
    spectral_columns = lax.iota(jnp.int32, bin_count) + 1
    sample_times = lax.iota(jnp.int32, length)
    phases = spectral_columns[:, None] * sample_times[None, :] % LISTEN_SPAN
    phase_angles = 2.0 * math.pi / LISTEN_SPAN * phases.astype(jnp.float32)
    inverse_root = 1.0 / math.sqrt(LISTEN_SPAN)
    return jnp.stack([jnp.cos(phase_angles) * inverse_root, -jnp.sin(phase_angles) * inverse_root], axis=1)

def inner_product(former, latter):
    return lax.dot_general(former, latter, (((1,), (1,)), ((), ())), precision=highest)

def outer_product(former, latter):
    return lax.dot_general(former, latter, (((0,), (0,)), ((), ())), precision=highest)

def reduce_rank(matrix, random_projector):
    real_part = matrix[0]
    imag_part = matrix[1]
    rank_count = random_projector.shape[1]
    proj_real = lax.dot_general(random_projector, real_part, (((0,), (1,)), ((), ())), precision=highest)
    proj_imag = lax.dot_general(random_projector, imag_part, (((0,), (1,)), ((), ())), precision=highest)
    gram_real = inner_product(proj_real, proj_real) + inner_product(proj_imag, proj_imag)
    gram_imag = inner_product(proj_real, proj_imag) - inner_product(proj_imag, proj_real)
    coef_real = jnp.dot(proj_real, real_part, precision=highest) + jnp.dot(proj_imag, imag_part, precision=highest)
    coef_imag = jnp.dot(proj_real, imag_part, precision=highest) - jnp.dot(proj_imag, real_part, precision=highest)
    system = jnp.concatenate([jnp.concatenate([gram_real, -gram_imag], 1), jnp.concatenate([gram_imag, gram_real], 1)], 0)
    ridge_shift = ridge_scale * jnp.trace(gram_real) / rank_count
    system = system + ridge_shift * jnp.eye(2 * rank_count, dtype=system.dtype)
    factor = jnp.linalg.cholesky(system)
    right_side = jnp.concatenate([coef_real, coef_imag], 0)
    halfway = lax.linalg.triangular_solve(factor, right_side, left_side=True, lower=True)
    solved = lax.linalg.triangular_solve(factor, halfway, left_side=True, lower=True, transpose_a=True)
    solution_real = solved[:rank_count]
    solution_imag = solved[rank_count:]
    low_real = outer_product(proj_real, solution_real) - outer_product(proj_imag, solution_imag)
    low_imag = outer_product(proj_real, solution_imag) + outer_product(proj_imag, solution_real)
    return jnp.stack([low_real, low_imag])

def reference(receiver_gathers, fourier_estimate, random_projector, release_sample):
    dft_rows = dft_table(FREQS, LISTEN_SPAN).reshape(2 * FREQS, LISTEN_SPAN)
    zero_extended = jnp.zeros((RECEIVER_COUNT, SOURCE_COUNT * SOURCE_SPACING + LISTEN_SPAN), jnp.float32)

    def place(record, source_label):
        source_start_moment = release_sample[source_label].astype(jnp.int32)
        coeffs = lax.dynamic_index_in_dim(fourier_estimate, source_label, 3, keepdims=False).reshape(2 * FREQS, RECEIVER_COUNT)
        window = 2.0 * lax.dot_general(coeffs, dft_rows, (((0,), (0,)), ((), ())), precision=highest)
        before = lax.dynamic_slice(record, (jnp.int32(0), source_start_moment), (RECEIVER_COUNT, LISTEN_SPAN))
        record = lax.dynamic_update_slice(record, before + window, (jnp.int32(0), source_start_moment))
        return (record, None)
    mixed_signal, unused = lax.scan(place, zero_extended, jnp.arange(SOURCE_COUNT, dtype=jnp.int32))
    misfit_signal = receiver_gathers - mixed_signal[:, :SOURCE_COUNT * SOURCE_SPACING]
    extended = jnp.concatenate([misfit_signal, jnp.zeros((RECEIVER_COUNT, LISTEN_SPAN), jnp.float32)], 1)

    def window_cut(source_label):
        source_start_moment = release_sample[source_label].astype(jnp.int32)
        window_piece = lax.dynamic_slice(extended, (jnp.int32(0), source_start_moment), (RECEIVER_COUNT, LISTEN_SPAN))
        return lax.dot_general(dft_rows, window_piece, (((1,), (1,)), ((), ())), precision=highest)
    adjoint_operator = lax.map(window_cut, jnp.arange(SOURCE_COUNT, dtype=jnp.int32))
    adjoint_operator = jnp.transpose(adjoint_operator.reshape(SOURCE_COUNT, FREQS, 2, RECEIVER_COUNT), (1, 2, 3, 0))
    updated = fourier_estimate + relaxation * adjoint_operator
    deblended = lax.map(partial(reduce_rank, random_projector=random_projector), updated)
    return (deblended, misfit_signal)
```

```python
import functools
import math

import jax
import jax.numpy as jnp
from jax import lax
from jax.experimental import pallas as pl
from jax.experimental.pallas import tpu as pltpu
from jax.sharding import PartitionSpec as P

LISTEN_SPAN = 4096
SOURCE_SPACING = 1024
LANES = 128
SPAN = LISTEN_SPAN // SOURCE_SPACING

relaxation = 0.25
ridge_scale = 0.001
highest = lax.Precision.HIGHEST


def inner_product(former, latter):
    return lax.dot_general(former, latter, (((1,), (1,)), ((), ())), precision=highest)


def outer_product(former, latter):
    return lax.dot_general(former, latter, (((0,), (0,)), ((), ())), precision=highest)


def reduce_rank(matrix, random_projector):
    real_part = matrix[0]
    imag_part = matrix[1]
    rank_count = random_projector.shape[1]
    proj_real = lax.dot_general(
        random_projector, real_part, (((0,), (1,)), ((), ())), precision=highest
    )
    proj_imag = lax.dot_general(
        random_projector, imag_part, (((0,), (1,)), ((), ())), precision=highest
    )
    gram_real = inner_product(proj_real, proj_real) + inner_product(proj_imag, proj_imag)
    gram_imag = inner_product(proj_real, proj_imag) - inner_product(proj_imag, proj_real)
    coef_real = jnp.dot(proj_real, real_part, precision=highest) + jnp.dot(
        proj_imag, imag_part, precision=highest
    )
    coef_imag = jnp.dot(proj_real, imag_part, precision=highest) - jnp.dot(
        proj_imag, real_part, precision=highest
    )
    system = jnp.concatenate(
        [jnp.concatenate([gram_real, -gram_imag], 1), jnp.concatenate([gram_imag, gram_real], 1)], 0
    )
    ridge_shift = ridge_scale * jnp.trace(gram_real) / rank_count
    system = system + ridge_shift * jnp.eye(2 * rank_count, dtype=system.dtype)
    right_side = jnp.concatenate([coef_real, coef_imag], 0)
    return system, right_side, proj_real, proj_imag


def restore(system, inverse, right_side, proj_real, proj_imag):
    rank_count = proj_real.shape[0]
    solved = jnp.dot(inverse, right_side, precision=highest)
    rest = right_side - jnp.dot(system, solved, precision=highest)
    solved = solved + jnp.dot(inverse, rest, precision=highest)
    solution_real = solved[:rank_count]
    solution_imag = solved[rank_count:]
    low_real = outer_product(proj_real, solution_real) - outer_product(proj_imag, solution_imag)
    low_imag = outer_product(proj_real, solution_imag) + outer_product(proj_imag, solution_real)
    return jnp.stack([low_real, low_imag])


def invert_kernel(system_ref, inverse_ref):
    count, size, _ = system_ref.shape
    held = [system_ref[m] for m in range(count)]
    lane = lax.broadcasted_iota(jnp.int32, (size, size), 1)
    line = lax.broadcasted_iota(jnp.int32, (size, size), 0)
    top = lax.broadcasted_iota(jnp.int32, (1, size), 1)
    for k in range(size):
        for m in range(count):
            a = held[m]
            pivot = 1.0 / a[k : k + 1, k : k + 1]
            row = jnp.where(top == k, pivot, a[k : k + 1, :] * pivot)
            rest = jnp.where(lane == k, 0.0, a) - a[:, k : k + 1] * row
            held[m] = jnp.where(line == k, row, rest)
    for m in range(count):
        inverse_ref[m] = held[m]


def pack_kernel(dims, src_ref, out_ref, flip):
    node_axis, freq_axis, nodes, shots, halo, per_row, rows, planes = dims
    parts = flip.shape[0]
    for part in range(parts):
        flip[part, :halo] = jnp.zeros((halo, LANES), jnp.float32)
    for plane in range(planes):
        for part in range(parts):
            flip[part, halo:] = src_ref[plane, part * LANES : (part + 1) * LANES].T
            for fb in range(freq_axis):
                picks = [
                    flip[part, pl.ds(fb * shots + i, rows, stride=per_row), :]
                    for i in range(per_row)
                ]
                for j in range(per_row):
                    nb = part * per_row + j
                    out_ref[nb * freq_axis + fb, plane * rows : (plane + 1) * rows, :] = (
                        jnp.concatenate([p[:, j * nodes : (j + 1) * nodes] for p in picks], 1)
                    )


def unpack_kernel(dims, packed_ref, src_ref, out_ref, flip):
    node_axis, freq_axis, nodes, shots, halo, per_row, rows, planes = dims
    parts = flip.shape[0]
    head = halo // per_row
    for plane in range(planes):
        for part in range(parts):
            for fb in range(freq_axis):
                pieces = [
                    packed_ref[
                        (part * per_row + j) * freq_axis + fb, plane * rows : (plane + 1) * rows, :
                    ]
                    for j in range(per_row)
                ]
                for i in range(per_row):
                    line = jnp.concatenate([p[:, i * nodes : (i + 1) * nodes] for p in pieces], 1)
                    start = fb * shots + i
                    if fb > 0:
                        at = pl.ds(start, head, stride=per_row)
                        flip[part, at, :] = flip[part, at, :] + line[:head]
                        flip[part, pl.ds(start + halo, rows - head, stride=per_row), :] = line[head:]
                    else:
                        flip[part, pl.ds(start, rows, stride=per_row), :] = line
            span = slice(part * LANES, (part + 1) * LANES)
            out_ref[plane, span] = src_ref[plane, span] + relaxation * flip[part, halo:].T


def swap_parts(x):
    even = lax.broadcasted_iota(jnp.int32, x.shape, 1) % 2 == 0
    width = x.shape[1]
    return jnp.where(even, pltpu.roll(x, width - 1, 1), pltpu.roll(x, 1, 1))


def split(x):
    hi = x.astype(jnp.bfloat16)
    return hi, (x - hi.astype(jnp.float32)).astype(jnp.bfloat16)


def split_table(x):
    hi = lax.reduce_precision(x, 8, 7)
    return hi.astype(jnp.bfloat16), (x - hi).astype(jnp.bfloat16)


def step_kernel(
    dims, per_step, dither, recv_ref, gather_ref, cos_ref, sin_ref, turn_ref, ahead_ref, back_ref,
    misfit_ref, packed_ref, coef, coef_swap, acc, frame,
):
    node_axis, freq_axis, nodes, shots, halo, per_row, rows, planes = dims
    bins = cos_ref.shape[1]
    step = pl.program_id(0)
    block = per_step * nodes

    @pl.when(step == 0)
    def _():
        acc[...] = jnp.zeros_like(acc)
        for r in range(rows):
            x = recv_ref[pl.ds(r, bins, stride=rows), :].T
            y = swap_parts(x)
            for i in range(per_row):
                l = r * per_row + i
                c = cos_ref[l : l + 1, :]
                s = sin_ref[l : l + 1, :]
                xi = x[i * nodes : (i + 1) * nodes]
                yi = y[i * nodes : (i + 1) * nodes]
                coef[l * nodes : (l + 1) * nodes] = xi * c + yi * s
                coef_swap[l * nodes : (l + 1) * nodes] = yi * c - xi * s

    base = step * per_step + halo
    def at(back):
        return pl.ds(pl.multiple_of((base - back) * nodes, nodes), block)

    steady = None
    for k in range(1, SPAN):
        a = turn_ref[k : k + 1, :]
        b = turn_ref[SPAN + k : SPAN + k + 1, :]
        term = coef[at(k), :] * a + coef_swap[at(k), :] * b
        steady = term if steady is None else steady + term
    hi, lo = split(jnp.concatenate([steady, coef[at(SPAN), :], coef[at(0), :]], 0))
    frame[...] = jnp.dot(
        jnp.concatenate([hi, lo, hi], 1), ahead_ref[...], preferred_element_type=jnp.float32
    )
    clock = lax.broadcasted_iota(jnp.int32, (1, SOURCE_SPACING), 1)
    full_hi, full_lo, old_hi, old_lo, new_hi, new_lo = [], [], [], [], [], []
    for i in range(per_step):
        leaving = clock < dither[base + i - SPAN]
        entering = clock >= dither[base + i]
        old_mask = leaving.astype(jnp.float32)
        new_mask = entering.astype(jnp.float32)
        row = slice(i * nodes, (i + 1) * nodes)
        mixed = (
            frame[i * nodes : (i + 1) * nodes]
            + frame[block + i * nodes : block + (i + 1) * nodes] * old_mask
            + frame[2 * block + i * nodes : 2 * block + (i + 1) * nodes] * new_mask
        )
        cols = slice(i * SOURCE_SPACING, (i + 1) * SOURCE_SPACING)
        misfit = gather_ref[:, cols] - mixed
        misfit_ref[:, cols] = misfit
        hi, lo = split(misfit)
        old_mask = old_mask.astype(jnp.bfloat16)
        new_mask = new_mask.astype(jnp.bfloat16)
        full_hi.append(hi)
        full_lo.append(lo)
        old_hi.append(hi * old_mask)
        old_lo.append(lo * old_mask)
        new_hi.append(hi * new_mask)
        new_lo.append(lo * new_mask)
    upper = jnp.concatenate(full_hi + old_hi + new_hi, 0)
    lower = jnp.concatenate(full_lo + old_lo + new_lo, 0)
    wide = jnp.dot(upper, back_ref[...], preferred_element_type=jnp.float32)
    narrow = jnp.dot(lower, back_ref[:, :bins], preferred_element_type=jnp.float32)
    total = wide[:, :bins] + wide[:, bins:] + narrow
    whole = total[:block]
    whole_swap = swap_parts(whole)
    for k in range(1, SPAN):
        a = turn_ref[k : k + 1, :]
        b = turn_ref[SPAN + k : SPAN + k + 1, :]
        acc[at(k), :] += whole * a - whole_swap * b
    acc[at(SPAN), :] += total[block : 2 * block]
    acc[at(0), :] += total[2 * block :]

    @pl.when(step == pl.num_programs(0) - 1)
    def _():
        for r in range(rows):
            x = acc[r * LANES : (r + 1) * LANES, :]
            y = swap_parts(x)
            parts = []
            for i in range(per_row):
                l = r * per_row + i
                c = cos_ref[l : l + 1, :]
                s = sin_ref[l : l + 1, :]
                parts.append(
                    x[i * nodes : (i + 1) * nodes] * c - y[i * nodes : (i + 1) * nodes] * s
                )
            packed_ref[pl.ds(r, bins, stride=rows), :] = jnp.concatenate(parts, 0).T


def shards(receiver_gathers, fourier_estimate, random_projector, release_sample):
    nodes, segment = receiver_gathers.shape
    freq_local, _, all_nodes, all_shots = fourier_estimate.shape
    shots = release_sample.shape[0]
    node_axis = lax.axis_size("node")
    freq_axis = lax.axis_size("freq")
    devices = node_axis * freq_axis
    planes = 2 * freq_local
    bins = planes * devices
    per_row = LANES // nodes
    rows = -(-(shots + SPAN) // per_row)
    while planes * rows % 8:
        rows += 1
    halo = rows * per_row - shots
    per_step = 8 if shots % 8 == 0 else 1
    dims = (node_axis, freq_axis, nodes, shots, halo, per_row, rows, planes)
    vmem = pltpu.VMEM
    whole = pl.BlockSpec(memory_space=vmem)
    params = pltpu.CompilerParams(vmem_limit_bytes=56 * 1024 * 1024)

    dither = release_sample % SOURCE_SPACING
    before = lax.ppermute(
        dither[shots - halo :], "freq", [(i, i + 1) for i in range(freq_axis - 1)]
    )
    dither = jnp.concatenate([before, dither])
    lane = lax.iota(jnp.int32, bins)
    column = lane // 2 + 1
    imag = lane % 2 == 1
    scale = 2.0 * math.pi / LISTEN_SPAN
    angle = scale * (dither[:, None] * column[None, :] % LISTEN_SPAN).astype(jnp.float32)
    cos_shift = jnp.cos(angle)
    sin_shift = jnp.where(imag[None, :], -jnp.sin(angle), jnp.sin(angle))
    quarter = column[None, :] * lax.iota(jnp.int32, SPAN)[:, None] % 4
    turn_same = jnp.where(quarter == 0, 1.0, jnp.where(quarter == 2, -1.0, 0.0))
    turn_cross = jnp.where(quarter == 1, -1.0, jnp.where(quarter == 3, 1.0, 0.0))
    turn_cross = jnp.where(imag[None, :], -turn_cross, turn_cross)
    turn = jnp.concatenate([turn_same, turn_cross], 0).astype(jnp.float32)
    clock = lax.iota(jnp.int32, SOURCE_SPACING)

    def table(phase, odd):
        theta = scale * (phase % LISTEN_SPAN).astype(jnp.float32)
        return jnp.where(odd, -jnp.sin(theta), jnp.cos(theta)) * (1.0 / math.sqrt(LISTEN_SPAN))

    ahead = table(column[:, None] * clock[None, :], imag[:, None])
    hi, lo = split_table(2.0 * ahead)
    ahead_table = jnp.concatenate([hi, hi, lo], 0)
    hi, lo = split_table(ahead.T)
    back_table = jnp.concatenate([hi, lo], 1)

    planar = fourier_estimate.reshape(planes, all_nodes, all_shots)
    packed = pl.pallas_call(
        functools.partial(pack_kernel, dims),
        out_shape=jax.ShapeDtypeStruct((devices, planes * rows, LANES), jnp.float32),
        in_specs=[whole],
        out_specs=whole,
        scratch_shapes=[vmem((all_nodes // LANES, halo + all_shots, LANES), jnp.float32)],
        compiler_params=params,
        name="pack",
    )(planar)
    arrived = lax.all_to_all(packed, ("node", "freq"), split_axis=0, concat_axis=0, tiled=True)
    width = per_step * SOURCE_SPACING
    misfit, spectra = pl.pallas_call(
        functools.partial(step_kernel, dims, per_step),
        grid=(shots // per_step,),
        out_shape=(
            jax.ShapeDtypeStruct((nodes, segment), jnp.float32),
            jax.ShapeDtypeStruct((bins * rows, LANES), jnp.float32),
        ),
        in_specs=[
            pl.BlockSpec(memory_space=pltpu.SMEM),
            whole,
            pl.BlockSpec((nodes, width), lambda i: (0, i)),
            whole,
            whole,
            whole,
            whole,
            whole,
        ],
        out_specs=(pl.BlockSpec((nodes, width), lambda i: (0, i)), whole),
        scratch_shapes=[
            vmem(((shots + halo) * nodes, bins), jnp.float32),
            vmem(((shots + halo) * nodes, bins), jnp.float32),
            vmem(((shots + halo) * nodes, bins), jnp.float32),
            vmem((3 * per_step * nodes, SOURCE_SPACING), jnp.float32),
        ],
        compiler_params=params,
        name="blend",
    )(
        dither, arrived.reshape(bins * rows, LANES), receiver_gathers, cos_shift, sin_shift, turn,
        ahead_table, back_table,
    )
    returned = lax.all_to_all(
        spectra.reshape(devices, planes * rows, LANES),
        ("node", "freq"),
        split_axis=0,
        concat_axis=0,
        tiled=True,
    )
    updated = pl.pallas_call(
        functools.partial(unpack_kernel, dims),
        out_shape=jax.ShapeDtypeStruct(planar.shape, jnp.float32),
        in_specs=[whole, whole],
        out_specs=whole,
        scratch_shapes=[vmem((all_nodes // LANES, halo + all_shots, LANES), jnp.float32)],
        compiler_params=params,
        name="unpack",
    )(returned, planar)
    updated = updated.reshape(fourier_estimate.shape)
    system, right_side, proj_real, proj_imag = jax.vmap(reduce_rank, in_axes=(0, None))(
        updated, random_projector
    )
    inverse = pl.pallas_call(
        invert_kernel,
        out_shape=jax.ShapeDtypeStruct(system.shape, jnp.float32),
        in_specs=[whole],
        out_specs=whole,
        compiler_params=params,
        name="invert",
    )(system)
    deblended = jax.vmap(restore)(system, inverse, right_side, proj_real, proj_imag)
    return (deblended, misfit)


def solution(mesh):
    return jax.shard_map(
        shards,
        mesh=mesh,
        in_specs=(P("node", "freq"), P(("node", "freq"), None, None, None), P(), P("freq")),
        out_specs=(P(("node", "freq"), None, None, None), P("node", "freq")),
        check_vma=False,
    )
```
